32 devices in a mesh: parts: 2 (over y), rows: 4 (over z), win: 2 (over x), rep: 2 (over core).
Axes of the slice: x: 2, y: 2, z: 4, core: 2. Of those that a mesh axis runs over, the one named last changes fastest.
Arguments:
- eig_upper: bfloat16 [196608, 2048], P(('parts', 'rows', 'rep'), 'win'), parts along dimension 0, may hold values from -0.01953125 to 0.01953125
- eig_lower: bfloat16 [196608, 2048], P(('parts', 'rows', 'rep'), 'win'), parts along dimension 0, may hold values from -6 to 6
- dipole: bfloat16 [768, 3, 256, 256], P(('parts', 'rows', 'rep')), parts along dimension 0, may hold values from -0.25 to 0.25
- block_cols: int32 [768, 3], P(('parts', 'rows', 'rep')), parts along dimension 0, may hold values from 0 to 383, as said below
- block_count: int32 [768], P(('parts', 'rows', 'rep')), parts along dimension 0, may hold values from 1 to 3, as said below
- energy_upper: float32 [4096], P(('parts', 'win')), parts along dimension 0, may hold values from 3 to 5
- energy_lower: float32 [4096], P(('parts', 'rows', 'rep')), parts along dimension 0, may hold values from 1 to 2
- sym_upper: int32 [4096], P(('parts', 'win')), parts along dimension 0, may hold values from 0 to 4
- sym_lower: int32 [4096], P(('parts', 'rows', 'rep')), parts along dimension 0, may hold values from 0 to 4
Outputs:
- einstein_a: float32 [4096, 2048], P(('parts', 'win'), ('rows', 'rep')), parts along dimension 0
- intensity: float32 [4096, 2048], P(('parts', 'win'), ('rows', 'rep')), parts along dimension 0
The draws below stay inside these ranges and needn't reach their ends.
There are 2 independent parts, one for each index of `parts`. The reference program is written for one: setup_inputs(seed, part) draws one part's arguments, and reference() takes and returns one part's arrays. A program takes and returns all parts, laid end to end along the dimension named above; each array names one. Nothing has to cross between parts.
Inputs may be any that keep to these rules, and one draw needn't show every extreme that they name: `block_cols`: slot 0 of block row b names b itself; every slot names a block within 4 of its row, and some row reaches 4; a row may name a block twice. `block_count`: some block row uses all 3 slots.
All inputs are finite; a program needn't handle non-finite values.
Results may differ from the reference program's by a relative error of at most 0.0033.
Values may be sent and summed in bfloat16 or wider, within the bound.
No kernel may reach another device: no remote copies, remote signals or barrier semaphores. Data moves between devices by JAX's collectives and lax.ppermute only.
A program may use at most 320 MiB of HBM per device.

```python
import jax
import jax.numpy as jnp
from jax import lax

NBR = 384
BLK = 256
MAXNZ = 3
BAND = 4
JUP = 21
NU = 2048
NL = 2048
NB = 98304
BR_DEV = 48


def edge_rows():
    row_ids = jnp.arange(NBR, dtype=jnp.int32)
    first_rows = (row_ids % BR_DEV == 0) & (row_ids >= BAND)
    last_rows = (row_ids % BR_DEV == BR_DEV - 1) & (row_ids + BAND < NBR)
    return (row_ids, first_rows, last_rows)


def draw_block_count(key, part):
    first_key, second_key = jax.random.split(jax.random.fold_in(key, 11))
    level = jax.random.randint(first_key, (NBR // BR_DEV,), 0, MAXNZ)
    base = jax.random.randint(second_key, (NBR,), 0, MAXNZ)
    counts = 1 + jnp.minimum(base, jnp.repeat(level, BR_DEV))
    row_ids, first_rows, last_rows = edge_rows()
    counts = jnp.where(first_rows, jnp.maximum(counts, 2), counts)
    counts = jnp.where(last_rows, MAXNZ, counts)
    counts = counts.at[0].set(MAXNZ)
    return counts.astype(jnp.int32)


def draw_block_cols(key, part):
    offsets = jax.random.randint(jax.random.fold_in(key, 23), (NBR, MAXNZ), -BAND, BAND + 1)
    offsets = offsets.at[:, 0].set(0)
    row_ids, first_rows, last_rows = edge_rows()
    rows_col = row_ids[:, None]
    columns = rows_col + offsets
    outside = (columns < 0) | (columns >= NBR)
    columns = jnp.where(outside, rows_col - offsets, columns)
    columns = columns.at[:, 1].set(jnp.where(first_rows, row_ids - BAND, columns[:, 1]))
    columns = columns.at[:, 2].set(jnp.where(last_rows, row_ids + BAND, columns[:, 2]))
    return columns.astype(jnp.int32)


def place_ends(entries, rng, smallest, top_value):
    index_at = [jax.random.randint(jax.random.fold_in(rng, axis), (), 0, length) for axis, length in enumerate(entries.shape)]
    longest = entries.shape.index(max(entries.shape))
    neighbour = index_at[:longest] + [(index_at[longest] + 1) % entries.shape[longest]] + index_at[longest + 1:]
    return entries.at[tuple(index_at)].set(smallest).at[tuple(neighbour)].set(top_value)


def block_levels(own_key, dims, cuts, least, top_value):
    def one(position, blocks):
        steps = jax.random.uniform(jax.random.fold_in(jax.random.fold_in(own_key, 6), position), (blocks,), jnp.float32, least / len(cuts), top_value / len(cuts))
        return jnp.repeat(jnp.exp(steps), dims[position] // blocks).reshape((-1,) + (1,) * (len(dims) - position - 1))

    gain = one(*cuts[0])
    for cut in cuts[1:]:
        gain = gain * one(*cut)
    return gain


def bell_draw(key, shape, scale, reach, shards=(), kind=jnp.bfloat16):
    loudness = block_levels(key, shape, shards, -0.22, 0.18) if shards else 1.0
    drawn = jax.random.normal(key, shape, jnp.float32) * scale * loudness
    return jnp.minimum(jnp.maximum(drawn, -reach), reach).astype(kind)


def setup_inputs(seed: int = 0, part: int = 0) -> dict:
    keys = jax.random.split(jax.random.key(seed), 10)
    own_keys = jax.random.split(jax.random.fold_in(keys[9], part), 10)
    eig_upper = bell_draw(own_keys[0], (NB, NU), NB ** -0.5, 0.01953125, ((0, 8), (1, 2)))
    eig_lower = bell_draw(own_keys[1], (NB, NL), 1.0, 6.0, ((0, 8), (1, 2)))
    dipole = bell_draw(own_keys[2], (NBR, MAXNZ, BLK, BLK), (2 * BLK) ** -0.5, 0.25, ((0, 8),))
    block_cols = draw_block_cols(jax.random.fold_in(jax.random.fold_in(keys[9], part), 71), part)
    block_count = draw_block_count(jax.random.fold_in(jax.random.fold_in(keys[9], part), 71), part)
    energy_upper = jnp.clip(3.0 + 2.0 * jax.random.uniform(own_keys[5], (NU,), jnp.float32) ** block_levels(own_keys[5], (NU,), ((0, 2),), -0.2, 0.2), 3.0, 5.0)
    energy_lower = jnp.clip(1.0 + 1.0 * jax.random.uniform(own_keys[6], (NL,), jnp.float32) ** block_levels(own_keys[6], (NL,), ((0, 8),), -0.2, 0.2), 1.0, 2.0)
    sym_upper = place_ends(jax.random.randint(own_keys[7], (NU,), 0, 5), jax.random.fold_in(own_keys[7], 1), 0, 4).astype(jnp.int32)
    sym_lower = place_ends(jax.random.randint(own_keys[8], (NL,), 0, 5), jax.random.fold_in(own_keys[8], 1), 0, 4).astype(jnp.int32)
    return dict(eig_upper=eig_upper, eig_lower=eig_lower, dipole=dipole, block_cols=block_cols, block_count=block_count, energy_upper=energy_upper, energy_lower=energy_lower, sym_upper=sym_upper, sym_lower=sym_lower)


EMISSION = 0.3136189
RADIATION = 0.71938845


def line_values(moments, energy_upper, energy_lower, sym_upper, sym_lower):
    wavenum = energy_upper[:, None] - energy_lower[None, :]
    partner = jnp.where(sym_upper == 2, 2, jnp.where(sym_upper < 2, 1 - sym_upper, 7 - sym_upper))
    allowed = (sym_lower[None, :] == partner[:, None]).astype(jnp.float32)
    spin_weight = jnp.where(sym_upper < 2, 5.0, jnp.where(sym_upper == 2, 2.0, 3.0)).astype(jnp.float32)
    degeneracy = 2.0 * JUP + 1.0
    einstein = allowed * EMISSION * wavenum ** 3 * moments * moments / degeneracy
    boltzmann = jnp.exp(-RADIATION * energy_lower[None, :])
    stimulated = 1.0 - jnp.exp(-RADIATION * wavenum)
    intensity = spin_weight[:, None] * degeneracy * einstein * boltzmann * stimulated / (wavenum * wavenum)
    return einstein, intensity


def reference(eig_upper, eig_lower, dipole, block_cols, block_count, energy_upper, energy_lower, sym_upper, sym_lower):
    lower_blocks = eig_lower.reshape(NBR, BLK, NL)

    def one_row(inputs):
        row_dipole, row_cols, row_count = inputs
        accumulated = jnp.zeros((BLK, NL), jnp.float32)
        for slot_index in range(MAXNZ):
            picked = lax.dynamic_index_in_dim(lower_blocks, row_cols[slot_index].astype(jnp.int32), 0, keepdims=False)
            live_mask = (row_count > slot_index).astype(jnp.float32)
            product = jnp.dot(row_dipole[slot_index], picked, preferred_element_type=jnp.float32)
            accumulated = accumulated + product * live_mask
        return accumulated.astype(jnp.bfloat16)

    lower_image = lax.map(one_row, (dipole, block_cols, block_count)).reshape(NBR * BLK, NL)
    moments = jnp.dot(eig_upper.T, lower_image, preferred_element_type=jnp.float32)
    return line_values(moments, energy_upper, energy_lower, sym_upper, sym_lower)
```

```python
import functools

import jax
import jax.numpy as jnp
from jax import lax
from jax.experimental import pallas as pl
from jax.experimental.pallas import tpu as pltpu
from jax.sharding import PartitionSpec as P

BAND = 4
JUP = 21


EMISSION = 0.3136189
RADIATION = 0.71938845
LANES = 128
TAIL = 2


def line_values(moments, energy_upper, energy_lower, sym_upper, sym_lower):
    wavenum = energy_upper[:, None] - energy_lower[None, :]
    partner = jnp.where(sym_upper == 2, 2, jnp.where(sym_upper < 2, 1 - sym_upper, 7 - sym_upper))
    allowed = (sym_lower[None, :] == partner[:, None]).astype(jnp.float32)
    spin_weight = jnp.where(sym_upper < 2, 5.0, jnp.where(sym_upper == 2, 2.0, 3.0)).astype(
        jnp.float32
    )
    degeneracy = 2.0 * JUP + 1.0
    einstein = allowed * EMISSION * wavenum**3 * moments * moments / degeneracy
    boltzmann = jnp.exp(-RADIATION * energy_lower[None, :])
    stimulated = 1.0 - jnp.exp(-RADIATION * wavenum)
    intensity = (
        spin_weight[:, None] * degeneracy * einstein * boltzmann * stimulated / (wavenum * wavenum)
    )
    return (einstein, intensity)


def image_kernel(slots, starts, where_ref, count_ref, turn_ref, dipole_ref, *refs):
    sources = refs[: 1 + 3 * (slots - 1)]
    outs, acc = refs[len(sources) : -1], refs[-1]
    row = pl.program_id(0)
    rows_here = pl.num_programs(0)
    acc[...] = jnp.dot(dipole_ref[0, 0], sources[0][...], preferred_element_type=jnp.float32)
    for slot in range(1, slots):
        place = where_ref[row * slots + slot]
        live = count_ref[row] > slot
        own, low, high = sources[1 + 3 * (slot - 1) : 4 + 3 * (slot - 1)]
        low_side, high_side = place < 0, place >= rows_here

        def add(ref, slot=slot):
            acc[...] += jnp.dot(dipole_ref[0, slot], ref[...], preferred_element_type=jnp.float32)

        pl.when(live & low_side)(functools.partial(add, low))
        pl.when(live & high_side)(functools.partial(add, high))
        pl.when(live & jnp.logical_not(low_side | high_side))(functools.partial(add, own))
    outs[0][...] = acc[...].astype(jnp.bfloat16)
    cols = acc.shape[1]
    for out, start in zip(outs[1:], starts):
        at = lax.rem(turn_ref[0] + start, cols)
        out[...] = outs[0][:, pl.ds(pl.multiple_of(at, LANES), LANES)]


def image(where_at, block_count, turn, dipole, lower, low, high, starts):
    rows_here, slots, size = dipole.shape[:3]
    cols = lower.shape[1]

    def at(slot, first, blocks):
        def index(row, where_ref, count_ref, turn_ref):
            return jnp.clip(where_ref[row * slots + slot] - first, 0, blocks - 1), 0

        return pl.BlockSpec((size, cols), index)

    by_row = lambda row, *_: (row, 0)
    specs = [
        pl.BlockSpec((1, slots, size, size), lambda row, *_: (row, 0, 0, 0)),
        pl.BlockSpec((size, cols), by_row),
    ]
    operands = [dipole, lower]
    for slot in range(1, slots):
        specs += [at(slot, 0, rows_here), at(slot, -BAND, BAND), at(slot, rows_here, BAND)]
        operands += [lower, low, high]
    out_specs = [pl.BlockSpec((size, cols), by_row)] + [pl.BlockSpec((size, LANES), by_row)] * len(starts)
    out_shape = [jax.ShapeDtypeStruct(lower.shape, jnp.bfloat16)] + [
        jax.ShapeDtypeStruct((lower.shape[0], LANES), jnp.bfloat16)
    ] * len(starts)
    return pl.pallas_call(
        functools.partial(image_kernel, slots, starts),
        grid_spec=pltpu.PrefetchScalarGridSpec(
            num_scalar_prefetch=3,
            grid=(rows_here,),
            in_specs=specs,
            out_specs=out_specs,
            scratch_shapes=[pltpu.VMEM((size, cols), jnp.float32)],
        ),
        out_shape=out_shape,
        compiler_params=pltpu.CompilerParams(vmem_limit_bytes=40 * 2**20),
        cost_estimate=pl.CostEstimate(
            flops=2 * rows_here * slots * size * size * cols,
            bytes_accessed=2 * rows_here * slots * size * (size + cols) + 4 * lower.size,
            transcendentals=0,
        ),
    )(where_at.reshape(-1), block_count, turn, *operands)


def halo(lower, width, axes):
    count = 1
    for axis in axes:
        count *= lax.axis_size(axis)
    up = [(i, i + 1) for i in range(count - 1)]
    down = [(i + 1, i) for i in range(count - 1)]
    low = lax.ppermute(lower[-width:], axes, up)
    high = lax.ppermute(lower[:width], axes, down)
    return low, high


def product(chunk, eig_upper):
    return lax.dot_general(
        chunk, eig_upper, (((0,), (0,)), ((), ())), preferred_element_type=jnp.float32
    )


def to_owner(partial, owner, rows, wins, reps):
    half = partial.shape[1] // reps
    rep = lax.axis_index("rep")
    mine = lax.dynamic_slice_in_dim(partial, rep * half, half, 1)
    for turn in range(1, reps):
        out = lax.dynamic_slice_in_dim(partial, (rep + turn) % reps * half, half, 1)
        mine = mine + lax.ppermute(out, "rep", [(i, (i + turn) % reps) for i in range(reps)])
    axes = ("rows", "win", "rep")
    place = lambda row, win, part: (row * wins + win) * reps + part
    pieces = []
    me = place(lax.axis_index("rows"), lax.axis_index("win"), rep)
    for part in range(reps):
        keep = functools.reduce(
            jnp.logical_or,
            [me == place(*owner(win)[:1], win, part) for win in range(wins) if owner(win)[1] == part],
            jnp.bool_(False),
        )
        total = jnp.where(keep, mine, 0.0)
        for turn in range(rows):
            pairs = []
            for win in range(wins):
                row, core = owner(win)
                if turn or core != part:
                    pairs.append((place((row + turn) % rows, win, part), place(row, win, core)))
            if pairs:
                total = total + lax.ppermute(mine, axes, pairs)
        pieces.append(total)
    return jnp.concatenate(pieces, axis=1)


def shards(
    eig_upper,
    eig_lower,
    dipole,
    block_cols,
    block_count,
    energy_upper,
    energy_lower,
    sym_upper,
    sym_lower,
):
    rows_here = dipole.shape[0]
    block_size = dipole.shape[2]
    cols = eig_lower.shape[1]
    share = energy_lower.shape[0]
    rows, wins, reps = (lax.axis_size(axis) for axis in ("rows", "win", "rep"))
    owners = ("rows", "rep")
    device = lax.axis_index(owners)
    win = lax.axis_index("win")
    chunks = cols // LANES
    tail = TAIL if wins == 2 and share == TAIL * LANES else 0
    turn_of = lambda w: (w * 2 // wins) * (cols // 2)

    where_at = block_cols - device * rows_here
    turn = turn_of(win)
    first = lax.dynamic_slice_in_dim(eig_lower, turn, LANES, 1)
    raw = [
        lax.ppermute(first, "win", [(i, (i + step) % wins) for i in range(wins)]) for step in range(1, wins)
    ]
    low, high = halo(eig_lower, BAND * block_size, owners)
    starts = tuple(LANES * i for i in range(1, chunks))
    whole, *sent = image(
        where_at, block_count, turn[None], dipole, eig_lower, low, high, starts
    )
    partials = jnp.zeros((cols * wins, eig_upper.shape[1]), jnp.float32)
    partials = lax.dynamic_update_slice_in_dim(partials, product(whole, eig_upper), win * cols, 0)
    late = []
    none = jnp.zeros((1,), jnp.int32)
    for step in range(1, wins):
        source = (win - step) % wins
        pairs = [(i, (i + step) % wins) for i in range(wins)]
        for index in range(chunks):
            if index:
                got = lax.ppermute(sent[index - 1], "win", pairs)
            else:
                ends = halo(raw[step - 1], BAND * block_size, owners)
                (got,) = image(where_at, block_count, none, dipole, raw[step - 1], *ends, ())
            part = product(got, eig_upper)
            if index < chunks - tail:
                at = source * cols + (turn_of(source) + index * LANES) % cols
                partials = lax.dynamic_update_slice_in_dim(partials, part, at, 0)
            else:

                def owner(w):
                    source = (w - step) % wins
                    at = source * cols + (turn_of(source) + index * LANES) % cols
                    return divmod(at // share, reps)

                late.append(to_owner(part, owner, rows, wins, reps))
    moments = lax.psum_scatter(partials, owners, scatter_dimension=0, tiled=True)
    if late:
        moments = moments + jnp.concatenate(late, axis=0)
    return line_values(moments.T, energy_upper, energy_lower, sym_upper, sym_lower)


def solution(mesh):
    in_specs = (
        P(("parts", "rows", "rep"), "win"),
        P(("parts", "rows", "rep"), "win"),
        P(("parts", "rows", "rep"), None, None, None),
        P(("parts", "rows", "rep"), None),
        P(("parts", "rows", "rep")),
        P(("parts", "win")),
        P(("parts", "rows", "rep")),
        P(("parts", "win")),
        P(("parts", "rows", "rep")),
    )
    out_specs = (P(("parts", "win"), ("rows", "rep")), P(("parts", "win"), ("rows", "rep")))
    return jax.shard_map(shards, mesh=mesh, in_specs=in_specs, out_specs=out_specs, check_vma=False)
```

```python
import functools

import jax
import jax.numpy as jnp
from jax import lax
from jax.experimental import pallas as pl
from jax.experimental.pallas import tpu as pltpu
from jax.sharding import PartitionSpec as P

BAND = 4
JUP = 21


EMISSION = 0.3136189
RADIATION = 0.71938845
LANES = 128
AXES = ("rows", "win", "rep")
VMEM = 60 * 2**20
SMALL = pl.CostEstimate(flops=1024, bytes_accessed=1024, transcendentals=0)


def image_kernel(slots, pieces, where_ref, count_ref, turn_ref, dipole_ref, *refs):
    sources = refs[: 1 + 3 * (slots - 1)]
    outs, acc = refs[len(sources) : -1], refs[-1]
    row = pl.program_id(0)
    rows_here = pl.num_programs(0)
    acc[...] = jnp.dot(dipole_ref[0, 0], sources[0][...], preferred_element_type=jnp.float32)
    for slot in range(1, slots):
        place = where_ref[row * slots + slot]
        live = count_ref[row] > slot
        own, low, high = sources[1 + 3 * (slot - 1) : 4 + 3 * (slot - 1)]
        low_side, high_side = place < 0, place >= rows_here

        def add(ref, slot=slot):
            acc[...] += jnp.dot(dipole_ref[0, slot], ref[...], preferred_element_type=jnp.float32)

        pl.when(live & low_side)(functools.partial(add, low))
        pl.when(live & high_side)(functools.partial(add, high))
        pl.when(live & jnp.logical_not(low_side | high_side))(functools.partial(add, own))
    outs[0][...] = acc[...].astype(jnp.bfloat16)
    cols = acc.shape[1]
    half = LANES // 2

    def tile(start):
        at = lax.rem(turn_ref[0] + start // LANES * LANES, cols)
        return acc[:, pl.ds(pl.multiple_of(at, LANES), LANES)]

    for out, (tiles, top, bottom) in zip(outs[1:], pieces):

        @pl.when((row >= top) & (row < bottom))
        def _(out=out, tiles=tiles):
            for index, starts in enumerate(tiles):
                value = tile(starts[0])
                if len(starts) > 1:
                    left = lax.broadcasted_iota(jnp.int32, value.shape, 1) < half
                    other = tile(starts[1])
                    if starts[0] % LANES:
                        value = pltpu.roll(value, half, 1)
                    else:
                        other = pltpu.roll(other, half, 1)
                    value = jnp.where(left, value, other)
                out[:, index * LANES : (index + 1) * LANES] = value.astype(jnp.bfloat16)


def image(where_at, block_count, turn, dipole, lower, low, high, pieces):
    rows_here, slots, size = dipole.shape[:3]
    cols = lower.shape[1]

    def at(slot, first, blocks):
        def index(row, where_ref, count_ref, turn_ref):
            return jnp.clip(where_ref[row * slots + slot] - first, 0, blocks - 1), 0

        return pl.BlockSpec((size, cols), index)

    by_row = lambda row, *_: (row, 0)
    specs = [
        pl.BlockSpec((1, slots, size, size), lambda row, *_: (row, 0, 0, 0)),
        pl.BlockSpec((size, cols), by_row),
    ]
    operands = [dipole, lower]
    for slot in range(1, slots):
        specs += [at(slot, 0, rows_here), at(slot, -BAND, BAND), at(slot, rows_here, BAND)]
        operands += [lower, low, high]
    out_specs = [pl.BlockSpec((size, cols), by_row)]
    out_shape = [jax.ShapeDtypeStruct(lower.shape, jnp.bfloat16)]
    for tiles, top, bottom in pieces:
        width = LANES * len(tiles)
        out_specs.append(
            pl.BlockSpec(
                (size, width),
                lambda row, *_, top=top, bottom=bottom: (jnp.clip(row, top, bottom - 1) - top, 0),
            )
        )
        out_shape.append(jax.ShapeDtypeStruct(((bottom - top) * size, width), jnp.bfloat16))
    return pl.pallas_call(
        functools.partial(image_kernel, slots, pieces),
        grid_spec=pltpu.PrefetchScalarGridSpec(
            num_scalar_prefetch=3,
            grid=(rows_here,),
            in_specs=specs,
            out_specs=out_specs,
            scratch_shapes=[pltpu.VMEM((size, cols), jnp.float32)],
        ),
        out_shape=out_shape,
        compiler_params=pltpu.CompilerParams(vmem_limit_bytes=VMEM),
        cost_estimate=SMALL,
    )(where_at.reshape(-1), block_count, turn, *operands)


def product_kernel(chunk_ref, upper_ref, out):
    @pl.when(pl.program_id(0) == 0)
    def _():
        out[...] = jnp.zeros_like(out)

    out[...] += lax.dot_general(
        chunk_ref[...], upper_ref[...], (((0,), (0,)), ((), ())), preferred_element_type=jnp.float32
    )


def product(chunk, eig_upper):
    depth, width = chunk.shape
    uppers = eig_upper.shape[1]
    step = 1024
    while depth % step:
        step //= 2
    return pl.pallas_call(
        product_kernel,
        grid=(depth // step,),
        in_specs=[pl.BlockSpec((step, width), lambda i: (i, 0)), pl.BlockSpec((step, uppers), lambda i: (i, 0))],
        out_specs=pl.BlockSpec((width, uppers), lambda i: (0, 0)),
        out_shape=jax.ShapeDtypeStruct((width, uppers), jnp.float32),
        compiler_params=pltpu.CompilerParams(vmem_limit_bytes=VMEM),
        cost_estimate=SMALL,
    )(chunk, eig_upper)


def part_product(chunk, eig_upper, first, given):
    part = lax.dot_general(
        chunk,
        eig_upper[first : first + chunk.shape[0]],
        (((0,), (0,)), ((), ())),
        preferred_element_type=jnp.float32,
    )
    return part if given is None else given + part


def lines_kernel(late, given, energy_upper, energy_lower, sym_upper, sym_lower, moments_ref, *refs):
    einstein_out, intensity_out = refs[-2:]
    moments = moments_ref[...]
    if late:
        parts = refs[given : given + late]
        total = parts[0][...].astype(jnp.float32)
        for part in parts[1:]:
            total = total + part[...].astype(jnp.float32)
        first = moments.shape[0] - total.shape[0]
        moments = jnp.concatenate([moments[:first], moments[first:] + total], axis=0)
    moments = moments.T
    label = sym_upper[...]
    partner = jnp.where(label == 2, 2, jnp.where(label < 2, 1 - label, 7 - label)).astype(jnp.float32)
    spin_weight = jnp.where(label < 2, 5.0, jnp.where(label == 2, 2.0, 3.0)).astype(jnp.float32)
    spread = lambda row: jnp.broadcast_to(row, (8, row.shape[1])).T[:, :1]
    upper, partner, spin_weight = spread(energy_upper[...]), spread(partner), spread(spin_weight)
    lower, other = energy_lower[...], sym_lower[...].astype(jnp.float32)
    wavenum = upper - lower
    degeneracy = 2.0 * JUP + 1.0
    strength = jnp.where(other == partner, EMISSION / degeneracy, 0.0) * (moments * moments) * wavenum
    boltzmann = jnp.exp(-RADIATION * lower)
    stimulated = 1.0 - jnp.exp(-RADIATION * wavenum)
    einstein_out[...] = strength * (wavenum * wavenum)
    intensity_out[...] = strength * (spin_weight * degeneracy) * (boltzmann * stimulated)


def lines(moments, late, first, count, outs, energy_upper, energy_lower, sym_upper, sym_lower):
    shape = (energy_upper.shape[0], energy_lower.shape[0])
    at = first // count
    full = lambda array: pl.BlockSpec(array.shape, lambda i: (0, 0))
    column = lambda height: pl.BlockSpec((height, count), lambda i: (0, at))
    operands = [energy_upper[None, :], energy_lower[None, :], sym_upper[None, :], sym_lower[None, :], moments]
    specs = [full(operands[0]), column(1), full(operands[2]), column(1)]
    specs += [full(moments)]
    specs += [pl.BlockSpec(memory_space=pl.ANY)] * len(outs) + [full(part) for part in late]
    return pl.pallas_call(
        functools.partial(lines_kernel, len(late), len(outs)),
        grid=(1,),
        in_specs=specs,
        out_specs=[column(shape[0])] * 2,
        out_shape=[jax.ShapeDtypeStruct(shape, jnp.float32)] * 2,
        input_output_aliases={len(operands) + i: i for i in range(len(outs))},
        compiler_params=pltpu.CompilerParams(vmem_limit_bytes=VMEM),
    )(*operands, *outs, *late)


def copy_kernel(at_ref, array_ref, out):
    out[...] = array_ref[...]


def columns(array, at, width):
    step = array.shape[0] // 6
    return pl.pallas_call(
        copy_kernel,
        grid_spec=pltpu.PrefetchScalarGridSpec(
            num_scalar_prefetch=1,
            grid=(6,),
            in_specs=[pl.BlockSpec((step, width), lambda i, at_ref: (i, at_ref[0]))],
            out_specs=pl.BlockSpec((step, width), lambda i, at_ref: (i, 0)),
        ),
        out_shape=jax.ShapeDtypeStruct((array.shape[0], width), array.dtype),
        compiler_params=pltpu.CompilerParams(vmem_limit_bytes=VMEM),
        cost_estimate=SMALL,
    )(at[None], array)


def halo(last, first, axes):
    count = 1
    for axis in axes:
        count *= lax.axis_size(axis)
    up = [(i, i + 1) for i in range(count - 1)]
    down = [(i + 1, i) for i in range(count - 1)]
    low = lax.ppermute(last, axes, up)
    high = lax.ppermute(first, axes, down)
    return low, high


def place(row, win, core):
    return (row * lax.axis_size("win") + win) * lax.axis_size("rep") + core


def to_chips(partial, groups, chip, wire=jnp.float32):
    rows, wins, reps = (lax.axis_size(axis) for axis in AXES)
    row, win, rep = (lax.axis_index(axis) for axis in AXES)
    split = partial.reshape(groups, reps, -1, partial.shape[1])
    of_core = lambda core: lax.dynamic_index_in_dim(split, core, 1, keepdims=False)
    mine = of_core(rep)
    for turn in range(1, reps):
        pairs = [(i, (i + turn) % reps) for i in range(reps)]
        mine = mine + lax.ppermute(of_core((rep + turn) % reps), "rep", pairs)
    first = functools.reduce(lambda at, w: jnp.where(win == w, chip(w), at), range(1, wins), chip(0))
    terms = []
    sent = mine.astype(wire)
    for turn in [*range(rows - 1, 0, -1), 0]:
        at = (row - turn - first) % rows
        piece = lax.dynamic_index_in_dim(sent if turn else mine, jnp.minimum(at, groups - 1), 0, keepdims=False)
        if turn:
            pairs = [
                (place((chip(w) + g + turn) % rows, w, core), place(chip(w) + g, w, core))
                for w in range(wins)
                for g in range(groups)
                for core in range(reps)
            ]
            terms.append(lax.ppermute(piece, AXES, pairs))
        else:
            terms.append(jnp.where(at < groups, piece, 0.0))
    return terms


def shards(
    eig_upper,
    eig_lower,
    dipole,
    block_cols,
    block_count,
    energy_upper,
    energy_lower,
    sym_upper,
    sym_lower,
):
    rows_here = dipole.shape[0]
    size = dipole.shape[2]
    cols = eig_lower.shape[1]
    depth = eig_lower.shape[0]
    uppers = eig_upper.shape[1]
    share = energy_lower.shape[0]
    rows, wins, reps = (lax.axis_size(axis) for axis in AXES)
    owners = ("rows", "rep")
    device = lax.axis_index(owners)
    row, win, rep = (lax.axis_index(axis) for axis in AXES)
    group = reps * share
    groups = cols // group
    chunks = group // LANES
    shift = lambda w: (w * 2 // wins) * (groups // 2)
    turn = shift(win) * group

    where_at = block_cols - device * rows_here
    none = jnp.zeros((1,), jnp.int32)
    raws = min(2, chunks)
    width = BAND * size
    first = columns(eig_lower, turn // (raws * LANES), raws * LANES)
    behind, first = lax.optimization_barrier((eig_lower, first))
    low, high = halo(behind[-width:], behind[:width], owners)

    tail = LANES // 2 if wins == 2 and reps == 2 and share == 2 * LANES else 0
    plan = [("raw", 0, (), 0, rows_here, (0, share) if raws == chunks else None)]
    for g in range(groups):
        start, end = g * group + (raws * LANES if g == 0 else 0), (g + 1) * group
        if tail and g == groups - 1:
            at = [start + core * share for core in range(reps)]
            plan.append(("whole", g, tuple((i,) for i in at), 0, rows_here, (0, LANES)))
            plan.append(("whole", g, (tuple(i + LANES for i in at),), 0, rows_here, (LANES, tail)))
            cuts = [0, rows_here * 5 // 8, rows_here * 7 // 8, rows_here]
            for top, bottom in zip(cuts, cuts[1:]):
                plan.append(("cut", g, (tuple(i + LANES + tail for i in at),), top, bottom, None))
            continue
        for at in range(start, end, 2 * LANES):
            tiles = tuple((i,) for i in range(at, min(at + 2 * LANES, end), LANES))
            plan.append(("whole", g, tiles, 0, rows_here, None))
        if start < end:
            plan[-1] = (*plan[-1][:-1], (0, share))
    whole, *sent = image(
        where_at, block_count, turn[None], dipole, eig_lower, low, high, tuple(item[2:5] for item in plan[1:])
    )
    own = product(whole, eig_upper)
    transfers = [
        (step, *item, array) for step in range(1, wins) for item, array in zip(plan, [first, *sent])
    ]
    count = len(transfers)
    got, late, waiting = [], [], []
    sums = {}
    summed = lambda last: [total for _, at, total in sums.values() if at <= last]

    def collect(part, groups, chip, when, start):
        terms = to_chips(part, groups, chip)
        sums[len(sums)] = start, when, functools.reduce(jnp.add, terms)

    def work(index, after):
        step, kind, g, _, top, bottom, batch, _ = transfers[index]
        piece, after, waiting[:] = lax.optimization_barrier((got[index], after, list(waiting)))

        def chip(w):
            source = (w - step) % wins
            return source * groups + (g + shift(source)) % groups

        if kind == "cut":
            part = part_product(piece, eig_upper, top * size, waiting.pop() if waiting else None)
            if bottom < rows_here:
                waiting.append(part)
            else:
                late.extend(to_chips(part, 1, chip, jnp.bfloat16))
            return part
        if kind == "raw":
            ends = halo(piece[-width:], piece[:width], owners)
            (piece,) = image(where_at, block_count, none, dipole, piece, *ends, ())
        part = product(piece, eig_upper)
        waiting.append(part)
        if batch:
            collect(jnp.concatenate(waiting, axis=0), 1, chip, index, batch[0])
            waiting.clear()
        return part

    def moments_of(first, many):
        total = jnp.zeros((many, uppers), jnp.float32)
        for start, _, term in sums.values():
            end = start + term.shape[0]
            low_end, high_end = max(start, first), min(end, first + many)
            if low_end < high_end:
                term = term[low_end - start : high_end - start]
                total = total + jnp.pad(term, ((low_end - first, first + many - high_end), (0, 0)))
        return total

    levels = (energy_upper, energy_lower, sym_upper, sym_lower)
    outs, rest = [], None
    for index in range(count + 2):
        ready = index - 2
        if ready == 0:
            collect(own, groups, lambda w: w * groups, 0, 0)
        if ready >= 0:
            after = summed(ready - 1) if ready > 1 else [own]
            if tail and ready == count - 2:
                outs = lines(moments_of(0, LANES), [], 0, LANES, [], *levels)
                rest = moments_of(LANES, LANES)
                after += [rest, *outs]
            made = work(ready, after)
        if index < count:
            step, *_, array = transfers[index]
            if ready >= 0:
                needs = got[ready] if transfers[ready][1] == "cut" else (got[ready], made)
                array, _ = lax.optimization_barrier((array, needs))
            got.append(lax.ppermute(array, "win", [(i, (i + step) % wins) for i in range(wins)]))
    if not tail:
        return tuple(lines(moments_of(0, share), [], 0, share, [], *levels))
    return tuple(lines(rest, late, LANES, LANES, outs, *levels))


def solution(mesh):
    in_specs = (
        P(("parts", "rows", "rep"), "win"),
        P(("parts", "rows", "rep"), "win"),
        P(("parts", "rows", "rep"), None, None, None),
        P(("parts", "rows", "rep"), None),
        P(("parts", "rows", "rep")),
        P(("parts", "win")),
        P(("parts", "rows", "rep")),
        P(("parts", "win")),
        P(("parts", "rows", "rep")),
    )
    out_specs = (P(("parts", "win"), ("rows", "rep")), P(("parts", "win"), ("rows", "rep")))
    return jax.shard_map(shards, mesh=mesh, in_specs=in_specs, out_specs=out_specs, check_vma=False)
```

```python
import functools

import jax
import jax.numpy as jnp
from jax import lax
from jax.experimental import pallas as pl
from jax.experimental.pallas import tpu as pltpu
from jax.sharding import PartitionSpec as P

BAND = 4
JUP = 21


EMISSION = 0.3136189
RADIATION = 0.71938845
LANES = 128
AXES = ("rows", "win", "rep")
VMEM = 60 * 2**20
SMALL = pl.CostEstimate(flops=1024, bytes_accessed=1024, transcendentals=0)


def image_kernel(slots, pieces, where_ref, count_ref, turn_ref, dipole_ref, *refs):
    sources = refs[: 1 + 3 * (slots - 1)]
    outs, acc = refs[len(sources) : -1], refs[-1]
    row = pl.program_id(0)
    rows_here = pl.num_programs(0)
    acc[...] = jnp.dot(dipole_ref[0, 0], sources[0][...], preferred_element_type=jnp.float32)
    for slot in range(1, slots):
        place = where_ref[row * slots + slot]
        live = count_ref[row] > slot
        own, low, high = sources[1 + 3 * (slot - 1) : 4 + 3 * (slot - 1)]
        low_side, high_side = place < 0, place >= rows_here

        def add(ref, slot=slot):
            acc[...] += jnp.dot(dipole_ref[0, slot], ref[...], preferred_element_type=jnp.float32)

        pl.when(live & low_side)(functools.partial(add, low))
        pl.when(live & high_side)(functools.partial(add, high))
        pl.when(live & jnp.logical_not(low_side | high_side))(functools.partial(add, own))
    outs[0][...] = acc[...].astype(jnp.bfloat16)
    cols = acc.shape[1]
    half = LANES // 2

    def tile(start):
        at = lax.rem(turn_ref[0] + start // LANES * LANES, cols)
        return acc[:, pl.ds(pl.multiple_of(at, LANES), LANES)]

    for out, (tiles, top, bottom) in zip(outs[1:], pieces):

        @pl.when((row >= top) & (row < bottom))
        def _(out=out, tiles=tiles):
            for index, starts in enumerate(tiles):
                value = tile(starts[0])
                if len(starts) > 1:
                    left = lax.broadcasted_iota(jnp.int32, value.shape, 1) < half
                    other = tile(starts[1])
                    if starts[0] % LANES:
                        value = pltpu.roll(value, half, 1)
                    else:
                        other = pltpu.roll(other, half, 1)
                    value = jnp.where(left, value, other)
                out[:, index * LANES : (index + 1) * LANES] = value.astype(jnp.bfloat16)


def image(where_at, block_count, turn, dipole, lower, low, high, pieces):
    rows_here, slots, size = dipole.shape[:3]
    cols = lower.shape[1]

    def at(slot, first, blocks):
        def index(row, where_ref, count_ref, turn_ref):
            return jnp.clip(where_ref[row * slots + slot] - first, 0, blocks - 1), 0

        return pl.BlockSpec((size, cols), index)

    by_row = lambda row, *_: (row, 0)
    specs = [
        pl.BlockSpec((1, slots, size, size), lambda row, *_: (row, 0, 0, 0)),
        pl.BlockSpec((size, cols), by_row),
    ]
    operands = [dipole, lower]
    for slot in range(1, slots):
        specs += [at(slot, 0, rows_here), at(slot, -BAND, BAND), at(slot, rows_here, BAND)]
        operands += [lower, low, high]
    out_specs = [pl.BlockSpec((size, cols), by_row)]
    out_shape = [jax.ShapeDtypeStruct(lower.shape, jnp.bfloat16)]
    for tiles, top, bottom in pieces:
        width = LANES * len(tiles)
        out_specs.append(
            pl.BlockSpec(
                (size, width),
                lambda row, *_, top=top, bottom=bottom: (jnp.clip(row, top, bottom - 1) - top, 0),
            )
        )
        out_shape.append(jax.ShapeDtypeStruct(((bottom - top) * size, width), jnp.bfloat16))
    return pl.pallas_call(
        functools.partial(image_kernel, slots, pieces),
        grid_spec=pltpu.PrefetchScalarGridSpec(
            num_scalar_prefetch=3,
            grid=(rows_here,),
            in_specs=specs,
            out_specs=out_specs,
            scratch_shapes=[pltpu.VMEM((size, cols), jnp.float32)],
        ),
        out_shape=out_shape,
        compiler_params=pltpu.CompilerParams(vmem_limit_bytes=VMEM),
        cost_estimate=SMALL,
    )(where_at.reshape(-1), block_count, turn, *operands)


def product_kernel(chunk_ref, upper_ref, out):
    @pl.when(pl.program_id(0) == 0)
    def _():
        out[...] = jnp.zeros_like(out)

    out[...] += lax.dot_general(
        chunk_ref[...], upper_ref[...], (((0,), (0,)), ((), ())), preferred_element_type=jnp.float32
    )


def product(chunk, eig_upper):
    depth, width = chunk.shape
    uppers = eig_upper.shape[1]
    step = 1024
    while depth % step:
        step //= 2
    return pl.pallas_call(
        product_kernel,
        grid=(depth // step,),
        in_specs=[pl.BlockSpec((step, width), lambda i: (i, 0)), pl.BlockSpec((step, uppers), lambda i: (i, 0))],
        out_specs=pl.BlockSpec((width, uppers), lambda i: (0, 0)),
        out_shape=jax.ShapeDtypeStruct((width, uppers), jnp.float32),
        compiler_params=pltpu.CompilerParams(vmem_limit_bytes=VMEM),
        cost_estimate=SMALL,
    )(chunk, eig_upper)


def part_product(chunk, eig_upper, first, given):
    part = lax.dot_general(
        chunk,
        eig_upper[first : first + chunk.shape[0]],
        (((0,), (0,)), ((), ())),
        preferred_element_type=jnp.float32,
    )
    return part if given is None else given + part


def lines_kernel(late, given, energy_upper, energy_lower, sym_upper, sym_lower, moments_ref, *refs):
    einstein_out, intensity_out = refs[-2:]
    moments = moments_ref[...]
    if late:
        parts = refs[given : given + late]
        total = parts[0][...].astype(jnp.float32)
        for part in parts[1:]:
            total = total + part[...].astype(jnp.float32)
        first = moments.shape[0] - total.shape[0]
        moments = jnp.concatenate([moments[:first], moments[first:] + total], axis=0)
    moments = moments.T
    label = sym_upper[...]
    partner = jnp.where(label == 2, 2, jnp.where(label < 2, 1 - label, 7 - label)).astype(jnp.float32)
    spin_weight = jnp.where(label < 2, 5.0, jnp.where(label == 2, 2.0, 3.0)).astype(jnp.float32)
    spread = lambda row: jnp.broadcast_to(row, (8, row.shape[1])).T[:, :1]
    upper, partner, spin_weight = spread(energy_upper[...]), spread(partner), spread(spin_weight)
    lower, other = energy_lower[...], sym_lower[...].astype(jnp.float32)
    wavenum = upper - lower
    degeneracy = 2.0 * JUP + 1.0
    strength = jnp.where(other == partner, EMISSION / degeneracy, 0.0) * (moments * moments) * wavenum
    boltzmann = jnp.exp(-RADIATION * lower)
    stimulated = 1.0 - jnp.exp(-RADIATION * wavenum)
    einstein_out[...] = strength * (wavenum * wavenum)
    intensity_out[...] = strength * (spin_weight * degeneracy) * (boltzmann * stimulated)


def lines(moments, late, first, count, outs, energy_upper, energy_lower, sym_upper, sym_lower):
    shape = (energy_upper.shape[0], energy_lower.shape[0])
    at = first // count
    full = lambda array: pl.BlockSpec(array.shape, lambda i: (0, 0))
    column = lambda height: pl.BlockSpec((height, count), lambda i: (0, at))
    operands = [energy_upper[None, :], energy_lower[None, :], sym_upper[None, :], sym_lower[None, :], moments]
    specs = [full(operands[0]), column(1), full(operands[2]), column(1)]
    specs += [full(moments)]
    specs += [pl.BlockSpec(memory_space=pl.ANY)] * len(outs) + [full(part) for part in late]
    return pl.pallas_call(
        functools.partial(lines_kernel, len(late), len(outs)),
        grid=(1,),
        in_specs=specs,
        out_specs=[column(shape[0])] * 2,
        out_shape=[jax.ShapeDtypeStruct(shape, jnp.float32)] * 2,
        input_output_aliases={len(operands) + i: i for i in range(len(outs))},
        compiler_params=pltpu.CompilerParams(vmem_limit_bytes=VMEM),
    )(*operands, *outs, *late)


def copy_kernel(at_ref, array_ref, out):
    out[...] = array_ref[...]


def columns(array, at, width):
    step = array.shape[0] // 2
    return pl.pallas_call(
        copy_kernel,
        grid_spec=pltpu.PrefetchScalarGridSpec(
            num_scalar_prefetch=1,
            grid=(2,),
            in_specs=[pl.BlockSpec((step, width), lambda i, at_ref: (i, at_ref[0]))],
            out_specs=pl.BlockSpec((step, width), lambda i, at_ref: (i, 0)),
        ),
        out_shape=jax.ShapeDtypeStruct((array.shape[0], width), array.dtype),
        compiler_params=pltpu.CompilerParams(vmem_limit_bytes=VMEM),
        cost_estimate=SMALL,
    )(at[None], array)


def halo(last, first, axes):
    count = 1
    for axis in axes:
        count *= lax.axis_size(axis)
    up = [(i, i + 1) for i in range(count - 1)]
    down = [(i + 1, i) for i in range(count - 1)]
    low = lax.ppermute(last, axes, up)
    high = lax.ppermute(first, axes, down)
    return low, high


def place(row, win, core):
    return (row * lax.axis_size("win") + win) * lax.axis_size("rep") + core


def of_chip(partial, groups):
    reps, rep = lax.axis_size("rep"), lax.axis_index("rep")
    split = partial.reshape(groups, reps, -1, partial.shape[1])
    of_core = lambda core: lax.dynamic_index_in_dim(split, core, 1, keepdims=False)
    mine = of_core(rep)
    for turn in range(1, reps):
        pairs = [(i, (i + turn) % reps) for i in range(reps)]
        mine = mine + lax.ppermute(of_core((rep + turn) % reps), "rep", pairs)
    return mine


def to_chips(partial, groups, chip):
    rows, wins, reps = (lax.axis_size(axis) for axis in AXES)
    row, win, _ = (lax.axis_index(axis) for axis in AXES)
    mine = of_chip(partial, groups)
    first = functools.reduce(lambda at, w: jnp.where(win == w, chip(w), at), range(1, wins), chip(0))
    terms = []
    for turn in [*range(rows - 1, 0, -1), 0]:
        at = (row - turn - first) % rows
        piece = lax.dynamic_index_in_dim(mine, jnp.minimum(at, groups - 1), 0, keepdims=False)
        if turn:
            pairs = [
                (place((chip(w) + g + turn) % rows, w, core), place(chip(w) + g, w, core))
                for w in range(wins)
                for g in range(groups)
                for core in range(reps)
            ]
            terms.append(lax.ppermute(piece, AXES, pairs))
        else:
            terms.append(jnp.where(at < groups, piece, 0.0))
    return terms


def to_chip(partial, chip):
    rows, wins, reps = (lax.axis_size(axis) for axis in AXES)
    row, win, _ = (lax.axis_index(axis) for axis in AXES)
    mine = of_chip(partial, 1)[0]
    sent = mine.astype(jnp.bfloat16)

    def sources(w):
        at = chip(w)
        rank = lambda other: (-abs(other - at), (other > at) != (2 * at < rows))
        return sorted((other for other in range(rows) if other != at), key=rank)

    terms = []
    for index in range(rows - 1):
        pairs = [
            (place(sources(w)[index], w, core), place(chip(w), w, core)) for w in range(wins) for core in range(reps)
        ]
        terms.append(lax.ppermute(sent, AXES, pairs))
    owner = functools.reduce(lambda at, w: jnp.where(win == w, chip(w), at), range(1, wins), chip(0))
    return [*terms, jnp.where(row == owner, mine, 0.0)]


def shards(
    eig_upper,
    eig_lower,
    dipole,
    block_cols,
    block_count,
    energy_upper,
    energy_lower,
    sym_upper,
    sym_lower,
):
    rows_here = dipole.shape[0]
    size = dipole.shape[2]
    cols = eig_lower.shape[1]
    depth = eig_lower.shape[0]
    uppers = eig_upper.shape[1]
    share = energy_lower.shape[0]
    rows, wins, reps = (lax.axis_size(axis) for axis in AXES)
    owners = ("rows", "rep")
    device = lax.axis_index(owners)
    row, win, rep = (lax.axis_index(axis) for axis in AXES)
    group = reps * share
    groups = cols // group
    chunks = group // LANES
    shift = lambda w: (w * 2 // wins) * (groups // 2)
    turn = shift(win) * group

    where_at = block_cols - device * rows_here
    none = jnp.zeros((1,), jnp.int32)
    raws = min(2, chunks)
    width = BAND * size
    first = columns(eig_lower, turn // (raws * LANES), raws * LANES)
    behind, first = lax.optimization_barrier((eig_lower, first))
    low, high = halo(behind[-width:], behind[:width], owners)

    tail = LANES // 2 if wins == 2 and reps == 2 and share == 2 * LANES else 0
    plan = [("raw", 0, (), 0, rows_here, (0, share) if raws == chunks else None)]
    for g in range(groups):
        start, end = g * group + (raws * LANES if g == 0 else 0), (g + 1) * group
        if tail and g == groups - 1:
            at = [start + core * share for core in range(reps)]
            plan.append(("whole", g, tuple((i,) for i in at), 0, rows_here, (0, LANES)))
            plan.append(("whole", g, (tuple(i + LANES for i in at),), 0, rows_here, (LANES, tail)))
            cuts = [0, rows_here * 13 // 16, rows_here]
            for top, bottom in zip(cuts, cuts[1:]):
                plan.append(("cut", g, (tuple(i + LANES + tail for i in at),), top, bottom, None))
            continue
        for at in range(start, end, 2 * LANES):
            tiles = tuple((i,) for i in range(at, min(at + 2 * LANES, end), LANES))
            plan.append(("whole", g, tiles, 0, rows_here, None))
        if start < end:
            plan[-1] = (*plan[-1][:-1], (0, share))
    whole, *sent = image(
        where_at, block_count, turn[None], dipole, eig_lower, low, high, tuple(item[2:5] for item in plan[1:])
    )
    own = product(whole, eig_upper)
    transfers = [
        (step, *item, array) for step in range(1, wins) for item, array in zip(plan, [first, *sent])
    ]
    count = len(transfers)
    got, late, waiting = [], [], []
    sums = {}
    summed = lambda last: [total for _, at, total in sums.values() if at <= last]

    def collect(part, groups, chip, when, start):
        terms = to_chips(part, groups, chip)
        sums[len(sums)] = start, when, functools.reduce(jnp.add, terms)

    def work(index, after):
        step, kind, g, _, top, bottom, batch, _ = transfers[index]
        piece, after, waiting[:] = lax.optimization_barrier((got[index], after, list(waiting)))

        def chip(w):
            source = (w - step) % wins
            return source * groups + (g + shift(source)) % groups

        if kind == "cut":
            part = part_product(piece, eig_upper, top * size, waiting.pop() if waiting else None)
            if bottom < rows_here:
                waiting.append(part)
            else:
                late.extend(to_chip(part, chip))
            return part
        if kind == "raw":
            ends = halo(piece[-width:], piece[:width], owners)
            (piece,) = image(where_at, block_count, none, dipole, piece, *ends, ())
        part = product(piece, eig_upper)
        waiting.append(part)
        if batch:
            collect(jnp.concatenate(waiting, axis=0), 1, chip, index, batch[0])
            waiting.clear()
        return part

    def moments_of(first, many):
        total = jnp.zeros((many, uppers), jnp.float32)
        for start, _, term in sums.values():
            end = start + term.shape[0]
            low_end, high_end = max(start, first), min(end, first + many)
            if low_end < high_end:
                term = term[low_end - start : high_end - start]
                total = total + jnp.pad(term, ((low_end - first, first + many - high_end), (0, 0)))
        return total

    levels = (energy_upper, energy_lower, sym_upper, sym_lower)
    outs, rest = [], None
    for index in range(count + 2):
        ready = index - 2
        if ready == 0:
            collect(own, groups, lambda w: w * groups, 0, 0)
        if ready >= 0:
            after = summed(ready - 1) if ready > 1 else [own]
            if tail and ready == count - 2:
                outs = lines(moments_of(0, LANES), [], 0, LANES, [], *levels)
                rest = moments_of(LANES, LANES)
                after += [rest, *outs]
            made = work(ready, after)
        if index < count:
            step, *_, array = transfers[index]
            if ready >= 0:
                needs = got[ready] if transfers[ready][1] == "cut" else (got[ready], made)
                array, _ = lax.optimization_barrier((array, needs))
            got.append(lax.ppermute(array, "win", [(i, (i + step) % wins) for i in range(wins)]))
    if not tail:
        return tuple(lines(moments_of(0, share), [], 0, share, [], *levels))
    return tuple(lines(rest, late, LANES, LANES, outs, *levels))


def solution(mesh):
    in_specs = (
        P(("parts", "rows", "rep"), "win"),
        P(("parts", "rows", "rep"), "win"),
        P(("parts", "rows", "rep"), None, None, None),
        P(("parts", "rows", "rep"), None),
        P(("parts", "rows", "rep")),
        P(("parts", "win")),
        P(("parts", "rows", "rep")),
        P(("parts", "win")),
        P(("parts", "rows", "rep")),
    )
    out_specs = (P(("parts", "win"), ("rows", "rep")), P(("parts", "win"), ("rows", "rep")))
    return jax.shard_map(shards, mesh=mesh, in_specs=in_specs, out_specs=out_specs, check_vma=False)
```

```python
import functools

import jax
import jax.numpy as jnp
from jax import lax
from jax.experimental import pallas as pl
from jax.experimental.pallas import tpu as pltpu
from jax.sharding import PartitionSpec as P

BAND = 4
JUP = 21


EMISSION = 0.3136189
RADIATION = 0.71938845
LANES = 128
AXES = ("rows", "win", "rep")
VMEM = 60 * 2**20
SMALL = pl.CostEstimate(flops=1024, bytes_accessed=1024, transcendentals=0)


def image_kernel(slots, pieces, where_ref, count_ref, turn_ref, dipole_ref, *refs):
    sources = refs[: 1 + 3 * (slots - 1)]
    outs, acc = refs[len(sources) : -1], refs[-1]
    row = pl.program_id(0)
    rows_here = pl.num_programs(0)
    acc[...] = jnp.dot(dipole_ref[0, 0], sources[0][...], preferred_element_type=jnp.float32)
    for slot in range(1, slots):
        place = where_ref[row * slots + slot]
        live = count_ref[row] > slot
        own, low, high = sources[1 + 3 * (slot - 1) : 4 + 3 * (slot - 1)]
        low_side, high_side = place < 0, place >= rows_here

        def add(ref, slot=slot):
            acc[...] += jnp.dot(dipole_ref[0, slot], ref[...], preferred_element_type=jnp.float32)

        pl.when(live & low_side)(functools.partial(add, low))
        pl.when(live & high_side)(functools.partial(add, high))
        pl.when(live & jnp.logical_not(low_side | high_side))(functools.partial(add, own))
    outs[0][...] = acc[...].astype(jnp.bfloat16)
    cols = acc.shape[1]
    half = LANES // 2

    def tile(start):
        at = lax.rem(turn_ref[0] + start // LANES * LANES, cols)
        return acc[:, pl.ds(pl.multiple_of(at, LANES), LANES)]

    for out, (tiles, top, bottom) in zip(outs[1:], pieces):

        @pl.when((row >= top) & (row < bottom))
        def _(out=out, tiles=tiles):
            for index, starts in enumerate(tiles):
                value = tile(starts[0])
                if len(starts) > 1:
                    left = lax.broadcasted_iota(jnp.int32, value.shape, 1) < half
                    other = tile(starts[1])
                    if starts[0] % LANES:
                        value = pltpu.roll(value, half, 1)
                    else:
                        other = pltpu.roll(other, half, 1)
                    value = jnp.where(left, value, other)
                out[:, index * LANES : (index + 1) * LANES] = value.astype(jnp.bfloat16)


def image(where_at, block_count, turn, dipole, lower, low, high, pieces):
    rows_here, slots, size = dipole.shape[:3]
    cols = lower.shape[1]

    def at(slot, first, blocks):
        def index(row, where_ref, count_ref, turn_ref):
            return jnp.clip(where_ref[row * slots + slot] - first, 0, blocks - 1), 0

        return pl.BlockSpec((size, cols), index)

    by_row = lambda row, *_: (row, 0)
    specs = [
        pl.BlockSpec((1, slots, size, size), lambda row, *_: (row, 0, 0, 0)),
        pl.BlockSpec((size, cols), by_row),
    ]
    operands = [dipole, lower]
    for slot in range(1, slots):
        specs += [at(slot, 0, rows_here), at(slot, -BAND, BAND), at(slot, rows_here, BAND)]
        operands += [lower, low, high]
    out_specs = [pl.BlockSpec((size, cols), by_row)]
    out_shape = [jax.ShapeDtypeStruct(lower.shape, jnp.bfloat16)]
    for tiles, top, bottom in pieces:
        width = LANES * len(tiles)
        out_specs.append(
            pl.BlockSpec(
                (size, width),
                lambda row, *_, top=top, bottom=bottom: (jnp.clip(row, top, bottom - 1) - top, 0),
            )
        )
        out_shape.append(jax.ShapeDtypeStruct(((bottom - top) * size, width), jnp.bfloat16))
    return pl.pallas_call(
        functools.partial(image_kernel, slots, pieces),
        grid_spec=pltpu.PrefetchScalarGridSpec(
            num_scalar_prefetch=3,
            grid=(rows_here,),
            in_specs=specs,
            out_specs=out_specs,
            scratch_shapes=[pltpu.VMEM((size, cols), jnp.float32)],
        ),
        out_shape=out_shape,
        compiler_params=pltpu.CompilerParams(vmem_limit_bytes=VMEM),
        cost_estimate=SMALL,
    )(where_at.reshape(-1), block_count, turn, *operands)


def product_kernel(chunk_ref, upper_ref, out):
    @pl.when(pl.program_id(0) == 0)
    def _():
        out[...] = jnp.zeros_like(out)

    out[...] += lax.dot_general(
        chunk_ref[...], upper_ref[...], (((0,), (0,)), ((), ())), preferred_element_type=jnp.float32
    )


def product(chunk, eig_upper):
    depth, width = chunk.shape
    uppers = eig_upper.shape[1]
    step = 1024
    while depth % step:
        step //= 2
    return pl.pallas_call(
        product_kernel,
        grid=(depth // step,),
        in_specs=[pl.BlockSpec((step, width), lambda i: (i, 0)), pl.BlockSpec((step, uppers), lambda i: (i, 0))],
        out_specs=pl.BlockSpec((width, uppers), lambda i: (0, 0)),
        out_shape=jax.ShapeDtypeStruct((width, uppers), jnp.float32),
        compiler_params=pltpu.CompilerParams(vmem_limit_bytes=VMEM),
        cost_estimate=SMALL,
    )(chunk, eig_upper)


def part_product(chunk, eig_upper, first, given):
    part = lax.dot_general(
        chunk,
        eig_upper[first : first + chunk.shape[0]],
        (((0,), (0,)), ((), ())),
        preferred_element_type=jnp.float32,
    )
    return part if given is None else given + part


def lines_kernel(late, given, energy_upper, energy_lower, sym_upper, sym_lower, moments_ref, *refs):
    einstein_out, intensity_out = refs[-2:]
    moments = moments_ref[...]
    if late:
        parts = refs[given : given + late]
        total = parts[0][...].astype(jnp.float32)
        for part in parts[1:]:
            total = total + part[...].astype(jnp.float32)
        first = moments.shape[0] - total.shape[0]
        moments = jnp.concatenate([moments[:first], moments[first:] + total], axis=0)
    moments = moments.T
    label = sym_upper[...]
    partner = jnp.where(label == 2, 2, jnp.where(label < 2, 1 - label, 7 - label)).astype(jnp.float32)
    spin_weight = jnp.where(label < 2, 5.0, jnp.where(label == 2, 2.0, 3.0)).astype(jnp.float32)
    spread = lambda row: jnp.broadcast_to(row, (8, row.shape[1])).T[:, :1]
    upper, partner, spin_weight = spread(energy_upper[...]), spread(partner), spread(spin_weight)
    lower, other = energy_lower[...], sym_lower[...].astype(jnp.float32)
    wavenum = upper - lower
    degeneracy = 2.0 * JUP + 1.0
    strength = jnp.where(other == partner, EMISSION / degeneracy, 0.0) * (moments * moments) * wavenum
    boltzmann = jnp.exp(-RADIATION * lower)
    stimulated = 1.0 - jnp.exp(-RADIATION * wavenum)
    einstein_out[...] = strength * (wavenum * wavenum)
    intensity_out[...] = strength * (spin_weight * degeneracy) * (boltzmann * stimulated)


def lines(moments, late, first, count, outs, energy_upper, energy_lower, sym_upper, sym_lower):
    shape = (energy_upper.shape[0], energy_lower.shape[0])
    at = first // count
    full = lambda array: pl.BlockSpec(array.shape, lambda i: (0, 0))
    column = lambda height: pl.BlockSpec((height, count), lambda i: (0, at))
    operands = [energy_upper[None, :], energy_lower[None, :], sym_upper[None, :], sym_lower[None, :], moments]
    specs = [full(operands[0]), column(1), full(operands[2]), column(1)]
    specs += [full(moments)]
    specs += [pl.BlockSpec(memory_space=pl.ANY)] * len(outs) + [full(part) for part in late]
    return pl.pallas_call(
        functools.partial(lines_kernel, len(late), len(outs)),
        grid=(1,),
        in_specs=specs,
        out_specs=[column(shape[0])] * 2,
        out_shape=[jax.ShapeDtypeStruct(shape, jnp.float32)] * 2,
        input_output_aliases={len(operands) + i: i for i in range(len(outs))},
        compiler_params=pltpu.CompilerParams(vmem_limit_bytes=VMEM),
    )(*operands, *outs, *late)


def copy_kernel(at_ref, array_ref, out):
    out[...] = array_ref[...]


def columns(array, at, width, first, steps, height):
    return pl.pallas_call(
        copy_kernel,
        grid_spec=pltpu.PrefetchScalarGridSpec(
            num_scalar_prefetch=1,
            grid=(steps,),
            in_specs=[pl.BlockSpec((height, width), lambda i, at_ref: (i + first, at_ref[0]))],
            out_specs=pl.BlockSpec((height, width), lambda i, at_ref: (i, 0)),
        ),
        out_shape=jax.ShapeDtypeStruct((steps * height, width), array.dtype),
        compiler_params=pltpu.CompilerParams(vmem_limit_bytes=VMEM),
        cost_estimate=SMALL,
    )(at[None], array)


def halo(last, first, axes):
    count = 1
    for axis in axes:
        count *= lax.axis_size(axis)
    up = [(i, i + 1) for i in range(count - 1)]
    down = [(i + 1, i) for i in range(count - 1)]
    low = lax.ppermute(last, axes, up)
    high = lax.ppermute(first, axes, down)
    return low, high


def place(row, win, core):
    return (row * lax.axis_size("win") + win) * lax.axis_size("rep") + core


def of_chip(partial, groups):
    reps, rep = lax.axis_size("rep"), lax.axis_index("rep")
    split = partial.reshape(groups, reps, -1, partial.shape[1])
    of_core = lambda core: lax.dynamic_index_in_dim(split, core, 1, keepdims=False)
    mine = of_core(rep)
    for turn in range(1, reps):
        pairs = [(i, (i + turn) % reps) for i in range(reps)]
        mine = mine + lax.ppermute(of_core((rep + turn) % reps), "rep", pairs)
    return mine


def to_chips(partial, groups, chip):
    rows, wins, reps = (lax.axis_size(axis) for axis in AXES)
    row, win, _ = (lax.axis_index(axis) for axis in AXES)
    mine = of_chip(partial, groups)
    first = functools.reduce(lambda at, w: jnp.where(win == w, chip(w), at), range(1, wins), chip(0))
    terms = []
    for turn in [*range(rows - 1, 0, -1), 0]:
        at = (row - turn - first) % rows
        piece = lax.dynamic_index_in_dim(mine, jnp.minimum(at, groups - 1), 0, keepdims=False)
        if turn:
            pairs = [
                (place((chip(w) + g + turn) % rows, w, core), place(chip(w) + g, w, core))
                for w in range(wins)
                for g in range(groups)
                for core in range(reps)
            ]
            terms.append(lax.ppermute(piece, AXES, pairs))
        else:
            terms.append(jnp.where(at < groups, piece, 0.0))
    return terms


def to_chip(partial, chip):
    rows, wins, reps = (lax.axis_size(axis) for axis in AXES)
    row, win, _ = (lax.axis_index(axis) for axis in AXES)
    mine = of_chip(partial, 1)[0]
    sent = mine.astype(jnp.bfloat16)

    def sources(w):
        at = chip(w)
        rank = lambda other: (-abs(other - at), (other > at) != (2 * at < rows))
        return sorted((other for other in range(rows) if other != at), key=rank)

    terms = []
    for index in range(rows - 1):
        pairs = [
            (place(sources(w)[index], w, core), place(chip(w), w, core)) for w in range(wins) for core in range(reps)
        ]
        terms.append(lax.ppermute(sent, AXES, pairs))
    owner = functools.reduce(lambda at, w: jnp.where(win == w, chip(w), at), range(1, wins), chip(0))
    return [*terms, jnp.where(row == owner, mine, 0.0)]


def shards(
    eig_upper,
    eig_lower,
    dipole,
    block_cols,
    block_count,
    energy_upper,
    energy_lower,
    sym_upper,
    sym_lower,
):
    rows_here = dipole.shape[0]
    size = dipole.shape[2]
    cols = eig_lower.shape[1]
    depth = eig_lower.shape[0]
    uppers = eig_upper.shape[1]
    share = energy_lower.shape[0]
    rows, wins, reps = (lax.axis_size(axis) for axis in AXES)
    owners = ("rows", "rep")
    device = lax.axis_index(owners)
    row, win, rep = (lax.axis_index(axis) for axis in AXES)
    group = reps * share
    groups = cols // group
    chunks = group // LANES
    shift = lambda w: (w * 2 // wins) * (groups // 2)
    turn = shift(win) * group

    where_at = block_cols - device * rows_here
    none = jnp.zeros((1,), jnp.int32)
    raws = min(2, chunks)
    width = BAND * size
    sixth = depth // 6
    at = turn // (raws * LANES)
    head = columns(eig_lower, at, raws * LANES, 0, 1, sixth)
    behind, head = lax.optimization_barrier((eig_lower, head))
    first = columns(behind, at, raws * LANES, 1, 5, sixth)
    over = lambda array, step: lax.ppermute(array, "win", [(i, (i + step) % wins) for i in range(wins)])
    heads = [over(head, step) for step in range(1, wins)]
    behind, heads[:1] = lax.optimization_barrier((behind, heads[:1]))
    low, high = halo(behind[-width:], behind[:width], owners)

    tail = LANES // 2 if wins == 2 and reps == 2 and share == 2 * LANES else 0
    plan = [("raw", 0, (), 0, rows_here, (0, share) if raws == chunks else None)]
    for g in range(groups):
        start, end = g * group + (raws * LANES if g == 0 else 0), (g + 1) * group
        if tail and g == groups - 1:
            at = [start + core * share for core in range(reps)]
            plan.append(("whole", g, tuple((i,) for i in at), 0, rows_here, (0, LANES)))
            plan.append(("whole", g, (tuple(i + LANES for i in at),), 0, rows_here, (LANES, tail)))
            cuts = [0, rows_here * 13 // 16, rows_here]
            for top, bottom in zip(cuts, cuts[1:]):
                plan.append(("cut", g, (tuple(i + LANES + tail for i in at),), top, bottom, None))
            continue
        for at in range(start, end, 2 * LANES):
            tiles = tuple((i,) for i in range(at, min(at + 2 * LANES, end), LANES))
            plan.append(("whole", g, tiles, 0, rows_here, None))
        if start < end:
            plan[-1] = (*plan[-1][:-1], (0, share))
    whole, *sent = image(
        where_at, block_count, turn[None], dipole, eig_lower, low, high, tuple(item[2:5] for item in plan[1:])
    )
    own = product(whole, eig_upper)
    transfers = [
        (step, *item, array) for step in range(1, wins) for item, array in zip(plan, [first, *sent])
    ]
    count = len(transfers)
    got, late, waiting = [], [], []
    sums = {}
    summed = lambda last: [total for _, at, total in sums.values() if at <= last]

    def collect(part, groups, chip, when, start):
        terms = to_chips(part, groups, chip)
        sums[len(sums)] = start, when, functools.reduce(jnp.add, terms)

    def work(index, after):
        step, kind, g, _, top, bottom, batch, _ = transfers[index]
        piece, after, waiting[:] = lax.optimization_barrier((got[index], after, list(waiting)))

        def chip(w):
            source = (w - step) % wins
            return source * groups + (g + shift(source)) % groups

        if kind == "cut":
            part = part_product(piece, eig_upper, top * size, waiting.pop() if waiting else None)
            if bottom < rows_here:
                waiting.append(part)
            else:
                late.extend(to_chip(part, chip))
            return part
        if kind == "raw":
            piece = jnp.concatenate([heads[step - 1], piece], axis=0)
            ends = halo(piece[-width:], piece[:width], owners)
            (piece,) = image(where_at, block_count, none, dipole, piece, *ends, ())
        part = product(piece, eig_upper)
        waiting.append(part)
        if batch:
            collect(jnp.concatenate(waiting, axis=0), 1, chip, index, batch[0])
            waiting.clear()
        return part

    def moments_of(first, many):
        total = jnp.zeros((many, uppers), jnp.float32)
        for start, _, term in sums.values():
            end = start + term.shape[0]
            low_end, high_end = max(start, first), min(end, first + many)
            if low_end < high_end:
                term = term[low_end - start : high_end - start]
                total = total + jnp.pad(term, ((low_end - first, first + many - high_end), (0, 0)))
        return total

    levels = (energy_upper, energy_lower, sym_upper, sym_lower)
    outs, rest = [], None
    for index in range(count + 2):
        ready = index - 2
        if ready == 0:
            collect(own, groups, lambda w: w * groups, 0, 0)
        if ready >= 0:
            after = summed(ready - 1) if ready > 1 else [own]
            if tail and ready == count - 2:
                outs = lines(moments_of(0, LANES), [], 0, LANES, [], *levels)
                rest = moments_of(LANES, LANES)
                after += [rest, *outs]
            made = work(ready, after)
        if index < count:
            step, *_, array = transfers[index]
            if ready >= 0:
                needs = got[ready] if transfers[ready][1] == "cut" else (got[ready], made)
                array, _ = lax.optimization_barrier((array, needs))
            got.append(over(array, step))
    if not tail:
        return tuple(lines(moments_of(0, share), [], 0, share, [], *levels))
    return tuple(lines(rest, late, LANES, LANES, outs, *levels))


def solution(mesh):
    in_specs = (
        P(("parts", "rows", "rep"), "win"),
        P(("parts", "rows", "rep"), "win"),
        P(("parts", "rows", "rep"), None, None, None),
        P(("parts", "rows", "rep"), None),
        P(("parts", "rows", "rep")),
        P(("parts", "win")),
        P(("parts", "rows", "rep")),
        P(("parts", "win")),
        P(("parts", "rows", "rep")),
    )
    out_specs = (P(("parts", "win"), ("rows", "rep")), P(("parts", "win"), ("rows", "rep")))
    return jax.shard_map(shards, mesh=mesh, in_specs=in_specs, out_specs=out_specs, check_vma=False)
```
